32 devices in a mesh: group: 4 (over y, x), dp: 2 (over core), mp: 4 (over z).
Axes of the slice: x: 2, y: 2, z: 4, core: 2. Of those that a mesh axis runs over, the one named last changes fastest.
Arguments:
- patches: bfloat16 [1024, 12800], P(('group', 'mp'), 'dp'), may hold values from -6 to 6
- norm_gain: float32 [12800], P('dp'), may hold values from 0.25 to 1.75
- norm_bias: float32 [12800], P('dp'), may hold values from -3 to 3
- proj_in: bfloat16 [12800, 4096], P('dp', ('group', 'mp')), may hold values from -0.0546875 to 0.0546875
- proj_in_bias: float32 [4096], P(('group', 'mp')), may hold values from -3 to 3
- proj_out: bfloat16 [4096, 4096], P(('group', 'mp'), 'dp'), may hold values from -0.09375 to 0.09375
- proj_out_bias: float32 [4096], P('dp'), may hold values from -3 to 3
- text_rows: bfloat16 [1024, 4096], P(('group', 'mp'), 'dp'), may hold values from -6 to 6
- out_grads: bfloat16 [1024, 4096], P(('group', 'mp'), 'dp'), may hold values from -6 to 6
- gate_weight: bfloat16 [4096, 14336], P('dp', 'mp'), may hold values from -0.09375 to 0.09375
- up_weight: bfloat16 [4096, 14336], P('dp', 'mp'), may hold values from -0.09375 to 0.09375
- down_weight: bfloat16 [14336, 4096], P('mp', 'dp'), may hold values from -0.046875 to 0.046875
- image_counts: int32 [16], replicated, may hold values from 16 to 64, as said below
- image_sequence: int32 [16], replicated, may hold values from 0 to 7, as said below
- image_offsets: int32 [16], replicated, may hold values from 0 to 112, as said below
Outputs:
- projected: bfloat16 [1024, 4096], P(('group', 'mp'), 'dp')
- sequence_grads: bfloat16 [1024, 4096], P(('group', 'mp'), 'dp')
- row_grads: bfloat16 [1024, 4096], P(('group', 'mp'), 'dp')
The draws below stay inside these ranges and needn't reach their ends.
Inputs may be any that keep to these rules, and one draw needn't show every extreme that they name: `image_counts`: image rows lie end to end from row 0 in image order; rows after the last image belong to no image. `image_sequence`: every sequence holds exactly two images. `image_offsets`: the two images of a sequence do not intersect and lie within its 128 rows.
All inputs are finite; a program needn't handle non-finite values.
Results may differ from the reference program's by a relative error of at most 0.0075.
Values may be sent and summed in bfloat16 or wider, within the bound.
A program may use at most 192 MiB of HBM per device.

```python
import jax
import jax.numpy as jnp
from jax import lax

FEAT = 12800
PROJ = 4096
D = 4096
FF = 14336
TOK_DEV = 128
IMAGES = 16
TOKENS = 1024


def image_plan(key):
    key = jax.random.fold_in(key, 11)
    first_key, order_key, gap_key, second_gap_key = jax.random.split(key, 4)
    counts = jax.random.randint(first_key, (IMAGES,), TOK_DEV // 8, TOK_DEV // 2 + 1).astype(jnp.int32)
    order = jax.random.permutation(order_key, IMAGES).astype(jnp.int32)
    counts = counts.at[order[1]].set(TOK_DEV // 8)
    counts = counts.at[order[2]].set(TOK_DEV // 2)
    slots = jnp.argsort(order, stable=True).astype(jnp.int32)
    sequence = (slots // 2).astype(jnp.int32)
    leading = order[0::2]
    trailing = order[1::2]
    lead_count = counts[leading]
    trail_count = counts[trailing]
    slack = TOK_DEV - lead_count - trail_count
    gap_one = jax.random.randint(gap_key, (IMAGES // 2,), 0, slack + 1).astype(jnp.int32)
    gap_one = gap_one.at[0].set(0)
    gap_two = jax.random.randint(second_gap_key, (IMAGES // 2,), 0, slack - gap_one + 1).astype(jnp.int32)
    gap_two = gap_two.at[0].set(slack[0])
    offsets = jnp.zeros((IMAGES,), jnp.int32)
    offsets = offsets.at[leading].set(gap_one)
    offsets = offsets.at[trailing].set(gap_one + lead_count + gap_two)
    return (counts, sequence, offsets)


def draw_image_counts(key, part):
    return image_plan(key)[0]


def draw_image_sequence(key, part):
    return image_plan(key)[1]


def draw_image_offsets(key, part):
    return image_plan(key)[2]


def levels(rng, extent, cuts, low, top_value):
    def one(position, shards_of):
        heights = jax.random.uniform(jax.random.fold_in(jax.random.fold_in(rng, 6), position), (shards_of,), jnp.float32, low / len(cuts), top_value / len(cuts))
        return jnp.repeat(jnp.exp(heights), extent[position] // shards_of).reshape((-1,) + (1,) * (len(extent) - position - 1))

    gain = one(*cuts[0])
    for cut in cuts[1:]:
        gain = gain * one(*cut)
    return gain


def scatter_about(stream_key, extent, scale, reach, cuts=(), kind=jnp.bfloat16):
    level = levels(stream_key, extent, cuts, -0.22, 0.18) if cuts else 1.0
    array = jax.random.normal(stream_key, extent, jnp.float32) * scale * level
    return jnp.minimum(jnp.maximum(array, -reach), reach).astype(kind)


def setup_inputs(seed: int = 0) -> dict:
    seeds = jax.random.split(jax.random.key(seed), 16)
    return {
        "patches": scatter_about(seeds[0], (TOKENS, FEAT), 1.0, 6.0, ((0, 16), (1, 2))),
        "norm_gain": jnp.clip(1.0 + 0.15 * jax.random.normal(seeds[1], (FEAT,), jnp.float32), 0.25, 1.75),
        "norm_bias": scatter_about(seeds[2], (FEAT,), 0.5, 3.0, ((0, 2),), jnp.float32),
        "proj_in": scatter_about(seeds[3], (FEAT, PROJ), FEAT ** -0.5, 0.0546875, ((0, 2), (1, 16))),
        "proj_in_bias": scatter_about(seeds[4], (PROJ,), 0.5, 3.0, ((0, 16),), jnp.float32),
        "proj_out": scatter_about(seeds[5], (PROJ, D), PROJ ** -0.5, 0.09375, ((0, 16), (1, 2))),
        "proj_out_bias": scatter_about(seeds[6], (D,), 0.5, 3.0, ((0, 2),), jnp.float32),
        "text_rows": scatter_about(seeds[7], (TOKENS, D), 1.0, 6.0, ((0, 16), (1, 2))),
        "out_grads": scatter_about(seeds[8], (TOKENS, D), 1.0, 6.0, ((0, 16), (1, 2))),
        "gate_weight": scatter_about(seeds[9], (D, FF), D ** -0.5, 0.09375, ((0, 2), (1, 4))),
        "up_weight": scatter_about(seeds[10], (D, FF), D ** -0.5, 0.09375, ((0, 2), (1, 4))),
        "down_weight": scatter_about(seeds[11], (FF, D), FF ** -0.5, 0.046875, ((0, 4), (1, 2))),
        "image_counts": draw_image_counts(jax.random.fold_in(seeds[15], 71), 0),
        "image_sequence": draw_image_sequence(jax.random.fold_in(seeds[15], 71), 0),
        "image_offsets": draw_image_offsets(jax.random.fold_in(seeds[15], 71), 0),
    }


def seq_sources(counts, sequence, offsets, length, first, count):
    starts = jnp.cumsum(counts) - counts
    rows = first + jnp.arange(count, dtype=jnp.int32)
    seq = rows // length
    pos = rows % length
    hit = (sequence[None, :] == seq[:, None]) & (offsets[None, :] <= pos[:, None]) & (pos[:, None] < (offsets + counts)[None, :])
    source = lax.optimization_barrier(jnp.sum(jnp.where(hit, starts[None, :] + pos[:, None] - offsets[None, :], 0), axis=1)).astype(jnp.int32)
    return (source, jnp.any(hit, axis=1))

def image_targets(counts, sequence, offsets, length, first, count):
    starts = jnp.cumsum(counts) - counts
    rows = first + jnp.arange(count, dtype=jnp.int32)
    hit = (starts[None, :] <= rows[:, None]) & (rows[:, None] < (starts + counts)[None, :])
    target = lax.optimization_barrier(jnp.sum(jnp.where(hit, sequence[None, :] * length + offsets[None, :] + rows[:, None] - starts[None, :], 0), axis=1)).astype(jnp.int32)
    return (target, jnp.any(hit, axis=1))

def reference(patches, norm_gain, norm_bias, proj_in, proj_in_bias, proj_out, proj_out_bias, text_rows, out_grads, gate_weight, up_weight, down_weight, image_counts, image_sequence, image_offsets):
    values = patches.astype(jnp.float32)
    mean = lax.optimization_barrier(jnp.mean(values, axis=1, keepdims=True))
    centred = values - mean
    spread = lax.optimization_barrier(jnp.mean(centred * centred, axis=1, keepdims=True))
    normed = (centred * jax.lax.rsqrt(spread + 1e-05) * norm_gain + norm_bias).astype(jnp.bfloat16)
    first = jnp.dot(normed, proj_in, preferred_element_type=jnp.float32) + proj_in_bias
    activated = jax.nn.gelu(first, approximate=False).astype(jnp.bfloat16)
    projected = (jnp.dot(activated, proj_out, preferred_element_type=jnp.float32) + proj_out_bias).astype(jnp.bfloat16)
    total = projected.shape[0]
    source, covered = seq_sources(image_counts, image_sequence, image_offsets, TOK_DEV, 0, total)
    inputs = jnp.where(covered[:, None], jnp.take(projected, source, axis=0), text_rows)
    gate = jnp.dot(inputs, gate_weight, preferred_element_type=jnp.float32)
    up = jnp.dot(inputs, up_weight, preferred_element_type=jnp.float32)
    hidden_grad = jnp.dot(out_grads, down_weight.T, preferred_element_type=jnp.float32)
    sig = jax.nn.sigmoid(gate)
    gate_grad = (hidden_grad * up * sig * (1.0 + gate * (1.0 - sig))).astype(jnp.bfloat16)
    up_grad = (hidden_grad * gate * sig).astype(jnp.bfloat16)
    input_grad = jnp.dot(gate_grad, gate_weight.T, preferred_element_type=jnp.float32) + jnp.dot(up_grad, up_weight.T, preferred_element_type=jnp.float32)
    sequence_grads = input_grad.astype(jnp.bfloat16)
    target, valid = image_targets(image_counts, image_sequence, image_offsets, TOK_DEV, 0, total)
    row_grads = jnp.where(valid[:, None], jnp.take(sequence_grads, target, axis=0), jnp.zeros((), jnp.bfloat16)).astype(jnp.bfloat16)
    return (projected, sequence_grads, row_grads)
```

```python
import functools

import jax
import jax.numpy as jnp
from jax import lax
from jax.sharding import PartitionSpec as P

TOK_DEV = 128


def seq_sources(counts, sequence, offsets, length, first, count):
    starts = jnp.cumsum(counts) - counts
    rows = first + jnp.arange(count, dtype=jnp.int32)
    seq = rows // length
    pos = rows % length
    hit = (
        (sequence[None, :] == seq[:, None])
        & (offsets[None, :] <= pos[:, None])
        & (pos[:, None] < (offsets + counts)[None, :])
    )
    source = jnp.sum(jnp.where(hit, starts[None, :] + pos[:, None] - offsets[None, :], 0), axis=1)
    return (source, jnp.any(hit, axis=1))


def image_targets(counts, sequence, offsets, length, first, count):
    starts = jnp.cumsum(counts) - counts
    rows = first + jnp.arange(count, dtype=jnp.int32)
    hit = (starts[None, :] <= rows[:, None]) & (rows[:, None] < (starts + counts)[None, :])
    target = jnp.sum(
        jnp.where(
            hit, sequence[None, :] * length + offsets[None, :] + rows[:, None] - starts[None, :], 0
        ),
        axis=1,
    )
    return (target, jnp.any(hit, axis=1))


def unit_grads(gate, up, hidden_grad):
    sig = jax.nn.sigmoid(gate)
    gate_grad = (hidden_grad * up * sig * (1.0 + gate * (1.0 - sig))).astype(jnp.bfloat16)
    up_grad = (hidden_grad * gate * sig).astype(jnp.bfloat16)
    return (gate_grad, up_grad)


def swap_dp(value):
    return lax.ppermute(value, "dp", [(0, 1), (1, 0)])


def half_rows(value, part):
    rows = value.shape[0] // 2
    return lax.dynamic_slice_in_dim(value, part * rows, rows, 0)


def local(
    sizes,
    patches,
    norm_gain,
    norm_bias,
    proj_in,
    proj_in_bias,
    proj_out,
    proj_out_bias,
    text_rows,
    out_grads,
    gate_weight,
    up_weight,
    down_weight,
    image_counts,
    image_sequence,
    image_offsets,
):
    groups, dps, mps = sizes
    devices = groups * mps
    local_rows, local_cols = text_rows.shape
    total = local_rows * devices
    group_rows = local_rows * mps
    group, dp, mp = (lax.axis_index(a) for a in ("group", "dp", "mp"))
    bf16, f32 = jnp.bfloat16, jnp.float32
    rank = ("mp", "group")

    block = local_cols // devices
    out_cols = lax.all_to_all(proj_out, rank, 1, 0, tiled=True)
    out_cols = lax.all_gather(out_cols, "dp", axis=1, tiled=True)
    out_bias = lax.dynamic_slice_in_dim(proj_out_bias, (mp * groups + group) * block, block, 0)
    out_bias = lax.all_gather(out_bias, "dp", axis=0, tiled=True)

    seq_text, seq_cotangent = (
        lax.all_gather(text_rows, "mp", axis=0, tiled=True),
        lax.all_gather(out_grads, "mp", axis=0, tiled=True),
    )

    values = patches.astype(f32)
    mean = lax.psum(jnp.sum(values, axis=1), "dp") / (patches.shape[1] * dps)
    centred = values - mean[:, None]
    spread = lax.psum(jnp.sum(centred * centred, axis=1), "dp") / (patches.shape[1] * dps)
    normed = (centred * lax.rsqrt(spread + 1e-05)[:, None] * norm_gain + norm_bias).astype(bf16)
    normed_all = lax.all_gather(normed, ("group", "mp"), axis=0, tiled=True)

    def matmul(a, b):
        return jnp.dot(a, b, preferred_element_type=f32)

    def matmul_t(a, b):
        return lax.dot_general(a, b, (((1,), (1,)), ((), ())), preferred_element_type=f32)

    def summed_share(value, op):
        if dps == 2:
            arriving = swap_dp(op(half_rows(value, 1 - dp)))
            return op(half_rows(value, dp)) + arriving
        return lax.psum_scatter(op(value), "dp", scatter_dimension=0, tiled=True)

    hidden_grad = summed_share(seq_cotangent, lambda rows: matmul_t(rows, down_weight))

    first = summed_share(normed_all, lambda rows: matmul(rows, proj_in))
    activated = jax.nn.gelu(first + proj_in_bias, approximate=False).astype(bf16)
    activated_all = lax.all_gather(activated, rank, axis=1, tiled=True)
    columns = (matmul(activated_all, out_cols) + out_bias).astype(bf16)
    columns = lax.all_to_all(columns, "dp", 1, 0, tiled=True)

    source, covered = seq_sources(
        image_counts, image_sequence, image_offsets, TOK_DEV, 0, total
    )
    placed = jnp.take(columns, source, axis=0)
    placed = lax.all_to_all(placed, "group", 0, 1, tiled=True)
    placed = lax.all_gather(placed, "mp", axis=1, tiled=True)
    covered = lax.dynamic_slice_in_dim(covered, group * group_rows, group_rows, 0)
    inputs = jnp.where(covered[:, None], placed, seq_text)

    by_rank = columns.reshape(groups, mps, local_rows, -1).swapaxes(0, 1).reshape(total, -1)
    projected = lax.all_to_all(by_rank, rank, 0, 1, tiled=True)

    up = summed_share(inputs, lambda rows: matmul(rows, up_weight))
    gate = summed_share(inputs, lambda rows: matmul(rows, gate_weight))
    gate_grad, up_grad = unit_grads(gate, up, hidden_grad)

    def back(gate_rows, up_rows):
        return (matmul_t(gate_rows, gate_weight) + matmul_t(up_rows, up_weight)).astype(bf16)

    if dps == 2:
        gate_other, up_other = swap_dp(gate_grad), swap_dp(up_grad)
        mine = back(gate_grad, up_grad)
        other = back(gate_other, up_other)
        partial = jnp.where(
            dp == 0, jnp.concatenate([mine, other], 0), jnp.concatenate([other, mine], 0)
        )
    else:
        partial = back(
            lax.all_gather(gate_grad, "dp", axis=0, tiled=True),
            lax.all_gather(up_grad, "dp", axis=0, tiled=True),
        )
    share = local_cols // mps
    shares = lax.all_to_all(
        partial.reshape(group_rows, mps, share).swapaxes(0, 1), "mp", 0, 0, tiled=True
    )
    grads = jnp.sum(shares.astype(f32), axis=0).astype(bf16)

    grads_all = lax.all_gather(grads, "group", axis=0, tiled=True)
    target, valid = image_targets(
        image_counts,
        image_sequence,
        image_offsets,
        TOK_DEV,
        group * group_rows,
        group_rows,
    )
    rows = jnp.where(valid[:, None], jnp.take(grads_all, target, axis=0), jnp.zeros((), bf16))
    row_grads = lax.all_to_all(rows, "mp", 0, 1, tiled=True)
    sequence_grads = lax.all_to_all(grads, "mp", 0, 1, tiled=True)
    return (projected, sequence_grads, row_grads)


def solution(mesh):
    sizes = tuple(mesh.shape[a] for a in ("group", "dp", "mp"))
    return jax.shard_map(
        functools.partial(local, sizes),
        mesh=mesh,
        in_specs=(
            P(("group", "mp"), "dp"),
            P("dp"),
            P("dp"),
            P("dp", ("group", "mp")),
            P(("group", "mp")),
            P(("group", "mp"), "dp"),
            P("dp"),
            P(("group", "mp"), "dp"),
            P(("group", "mp"), "dp"),
            P("dp", "mp"),
            P("dp", "mp"),
            P("mp", "dp"),
            P(),
            P(),
            P(),
        ),
        out_specs=(P(("group", "mp"), "dp"), P(("group", "mp"), "dp"), P(("group", "mp"), "dp")),
        check_vma=False,
    )
```

```python
import functools

import jax
import jax.numpy as jnp
from jax import lax
from jax.experimental import pallas as pl
from jax.experimental.pallas import tpu as pltpu
from jax.sharding import PartitionSpec as P

TOK_DEV = 128


def seq_sources(counts, sequence, offsets, length, first, count):
    starts = jnp.cumsum(counts) - counts
    rows = first + jnp.arange(count, dtype=jnp.int32)
    seq = rows // length
    pos = rows % length
    hit = (
        (sequence[None, :] == seq[:, None])
        & (offsets[None, :] <= pos[:, None])
        & (pos[:, None] < (offsets + counts)[None, :])
    )
    source = jnp.sum(jnp.where(hit, starts[None, :] + pos[:, None] - offsets[None, :], 0), axis=1)
    return (source, jnp.any(hit, axis=1))


def image_targets(counts, sequence, offsets, length, first, count):
    starts = jnp.cumsum(counts) - counts
    rows = first + jnp.arange(count, dtype=jnp.int32)
    hit = (starts[None, :] <= rows[:, None]) & (rows[:, None] < (starts + counts)[None, :])
    target = jnp.sum(
        jnp.where(
            hit, sequence[None, :] * length + offsets[None, :] + rows[:, None] - starts[None, :], 0
        ),
        axis=1,
    )
    return (target, jnp.any(hit, axis=1))


def unit_grads(gate, up, hidden_grad):
    sig = jax.nn.sigmoid(gate)
    gate_grad = (hidden_grad * up * sig * (1.0 + gate * (1.0 - sig))).astype(jnp.bfloat16)
    up_grad = (hidden_grad * gate * sig).astype(jnp.bfloat16)
    return (gate_grad, up_grad)


def gather_kernel(groups, mps, x_ref, out_ref, local_sem, send_sem, recv_sem):
    g, m = lax.axis_index("group"), lax.axis_index("mp")
    gx = g + 1 - 2 * (g % 2)
    gy = g + 2 - 4 * (g // 2)
    gd = 3 - g
    rows, width = x_ref.shape
    cut, half = rows - rows // 4, width // 2
    head, tail = pl.ds(0, cut), pl.ds(cut, rows - cut)
    every, left, right = pl.ds(0, width), pl.ds(0, half), pl.ds(half, width - half)
    slots, sent = {}, []
    to_x, to_y = {"group": gx}, {"group": gy}
    low, high = {"mp": m - 1}, {"mp": m + 1}

    def slot(key):
        return slots.setdefault(key, len(slots))

    def send(key, owner, line, part, cols, target, when=None, own=False):
        dst = out_ref.at[owner, line, part, cols]
        copy = pltpu.make_async_remote_copy(
            src_ref=x_ref.at[part, cols] if own else dst,
            dst_ref=dst,
            send_sem=send_sem.at[slot(key)],
            recv_sem=recv_sem.at[slot(key)],
            device_id=target,
            device_id_type=pl.DeviceIdType.MESH,
        )
        guarded(when, copy.start)
        sent.append((when, copy))

    def arrive(key, owner, line, part, cols, source, when=None):
        dst = out_ref.at[owner, line, part, cols]
        copy = pltpu.make_async_remote_copy(
            src_ref=dst,
            dst_ref=dst,
            send_sem=send_sem.at[slot(key)],
            recv_sem=recv_sem.at[slot(key)],
            device_id=source,
            device_id_type=pl.DeviceIdType.MESH,
        )
        guarded(when, copy.wait_recv)

    def guarded(when, act):
        if when is None:
            act()
        else:
            pl.when(when)(lambda: act())

    barrier = pltpu.get_barrier_semaphore()
    has_low, has_high = m > 0, m < mps - 1

    def greet(target):
        pl.semaphore_signal(
            barrier, inc=1, device_id=target, device_id_type=pl.DeviceIdType.MESH
        )

    greet(to_x)
    greet(to_y)
    guarded(has_low, lambda: greet(low))
    guarded(has_high, lambda: greet(high))
    pl.semaphore_wait(barrier, 2 + (m + mps - 1) // mps + (2 * mps - 2 - m) // mps)

    keep = pltpu.make_async_copy(x_ref, out_ref.at[g, m], local_sem)
    keep.start()
    send(("up", 0), g, m, head, every, high, has_high, True)
    send(("down", 0), g, m, head, every, low, has_low, True)
    send("tail_x", g, m, tail, every, to_x, None, True)
    send("tail_y", g, m, tail, every, to_y, None, True)
    send(("x", 0, 0), g, m, head, every, to_x, None, True)
    send(("y", 0, 0), g, m, head, every, to_y, None, True)
    send(("up", 0, 0), g, m, tail, every, high, has_high, True)
    send(("down", 0, 0), g, m, tail, every, low, has_low, True)

    arrive("tail_x", gx, m, tail, every, to_x)
    send("tail_xy", gx, m, tail, left, to_y)
    arrive("tail_y", gy, m, tail, every, to_y)
    send("tail_yx", gy, m, tail, right, to_x)
    for owner, j in ((gx, 1), (gy, 2)):
        send(("up", 0, j), owner, m, tail, every, high, has_high)
        send(("down", 0, j), owner, m, tail, every, low, has_low)
    arrive("tail_xy", gd, m, tail, left, to_y)
    arrive("tail_yx", gd, m, tail, right, to_x)
    send(("up", 0, 3), gd, m, tail, every, high, has_high)
    send(("down", 0, 3), gd, m, tail, every, low, has_low)

    def turn(key, line, when=None):
        arrive(("x",) + key, gx, line, head, every, to_x, when)
        send(("xy",) + key, gx, line, head, left, to_y, when)
        arrive(("y",) + key, gy, line, head, every, to_y, when)
        send(("yx",) + key, gy, line, head, right, to_x, when)

    turn((0, 0), m)
    lines = [((0, 0), m, None)]
    for step in range(1, mps):
        ways = (
            ("up", m - step, m >= step, low, high, (m >= step) & has_high),
            ("down", m + step, m < mps - step, high, low, (m < mps - step) & has_low),
        )
        for name, line, come, source, target, on in ways:
            arrive((name, step - 1), g, line, head, every, source, come)
            if step < mps - 1:
                send((name, step), g, line, head, every, target, on)
            send(("x", name, step), g, line, head, every, to_x, come)
            send(("y", name, step), g, line, head, every, to_y, come)
        for name, line, come, source, target, on in ways:
            for owner, j in ((g, 0), (gx, 1), (gy, 2), (gd, 3)):
                arrive((name, step - 1, j), owner, line, tail, every, source, come)
                if step < mps - 1:
                    send((name, step, j), owner, line, tail, every, target, on)
        for name, line, come, source, target, on in ways:
            turn((name, step), line, come)
            lines.append(((name, step), line, come))
    for key, line, come in lines:
        arrive(("xy",) + key, gd, line, head, left, to_y, come)
        arrive(("yx",) + key, gd, line, head, right, to_x, come)
    for when, copy in sent:
        guarded(when, copy.wait_send)
    keep.wait()


def gather_blocks(value, groups, mps, ident):
    rows, width = value.shape
    if groups != 4 or mps < 2 or rows % 64 or width % 256:
        whole = lax.all_gather(value, ("group", "mp"), axis=0, tiled=False)
        return whole.reshape(groups, mps, rows, width)
    count = 4 + 2 * (mps - 1) * 5 + 4 * (2 * mps - 1)
    return pl.pallas_call(
        functools.partial(gather_kernel, groups, mps),
        out_shape=jax.ShapeDtypeStruct((groups, mps, rows, width), value.dtype),
        in_specs=[pl.BlockSpec(memory_space=pl.ANY)],
        out_specs=pl.BlockSpec(memory_space=pl.ANY),
        scratch_shapes=[
            pltpu.SemaphoreType.DMA(()),
            pltpu.SemaphoreType.DMA((count,)),
            pltpu.SemaphoreType.DMA((count,)),
        ],
        compiler_params=pltpu.CompilerParams(collective_id=ident, has_side_effects=True),
        cost_estimate=pl.CostEstimate(
            flops=0, bytes_accessed=2 * groups * mps * rows * width * 2, transcendentals=0
        ),
    )(value)


def swap_dp(value):
    return lax.ppermute(value, "dp", [(0, 1), (1, 0)])


def half_rows(value, part):
    rows = value.shape[0] // 2
    return lax.dynamic_slice_in_dim(value, part * rows, rows, 0)


def local(
    sizes,
    patches,
    norm_gain,
    norm_bias,
    proj_in,
    proj_in_bias,
    proj_out,
    proj_out_bias,
    text_rows,
    out_grads,
    gate_weight,
    up_weight,
    down_weight,
    image_counts,
    image_sequence,
    image_offsets,
):
    groups, dps, mps = sizes
    devices = groups * mps
    local_rows, local_cols = text_rows.shape
    total = local_rows * devices
    group_rows = local_rows * mps
    group, dp, mp = (lax.axis_index(a) for a in ("group", "dp", "mp"))
    bf16, f32 = jnp.bfloat16, jnp.float32
    rank = ("mp", "group")

    block = local_cols // devices
    out_cols = lax.all_to_all(proj_out, rank, 1, 0, tiled=True)
    out_cols = lax.all_gather(out_cols, "dp", axis=1, tiled=True)
    out_bias = lax.dynamic_slice_in_dim(proj_out_bias, (mp * groups + group) * block, block, 0)
    out_bias = lax.all_gather(out_bias, "dp", axis=0, tiled=True)

    seq_text, seq_cotangent = (
        lax.all_gather(text_rows, "mp", axis=0, tiled=True),
        lax.all_gather(out_grads, "mp", axis=0, tiled=True),
    )

    values = patches.astype(f32)
    mean = lax.psum(jnp.sum(values, axis=1), "dp") / (patches.shape[1] * dps)
    centred = values - mean[:, None]
    spread = lax.psum(jnp.sum(centred * centred, axis=1), "dp") / (patches.shape[1] * dps)
    normed = (centred * lax.rsqrt(spread + 1e-05)[:, None] * norm_gain + norm_bias).astype(bf16)
    normed_all = gather_blocks(normed, groups, mps, 0).reshape(total, -1)

    def matmul(a, b):
        return jnp.dot(a, b, preferred_element_type=f32)

    def matmul_t(a, b):
        return lax.dot_general(a, b, (((1,), (1,)), ((), ())), preferred_element_type=f32)

    def summed_share(value, op):
        if dps == 2:
            arriving = swap_dp(op(half_rows(value, 1 - dp)))
            return op(half_rows(value, dp)) + arriving
        return lax.psum_scatter(op(value), "dp", scatter_dimension=0, tiled=True)

    hidden_grad = summed_share(seq_cotangent, lambda rows: matmul_t(rows, down_weight))

    first = summed_share(normed_all, lambda rows: matmul(rows, proj_in))
    activated = jax.nn.gelu(first + proj_in_bias, approximate=False).astype(bf16)
    activated_all = gather_blocks(activated, groups, mps, 1).transpose(2, 1, 0, 3)
    activated_all = activated_all.reshape(activated.shape[0], -1)
    columns = (matmul(activated_all, out_cols) + out_bias).astype(bf16)
    columns = lax.all_to_all(columns, "dp", 1, 0, tiled=True)

    source, covered = seq_sources(
        image_counts, image_sequence, image_offsets, TOK_DEV, 0, total
    )
    placed = jnp.take(columns, source, axis=0)
    placed = lax.all_to_all(placed, "group", 0, 1, tiled=True)
    placed = lax.all_gather(placed, "mp", axis=1, tiled=True)
    covered = lax.dynamic_slice_in_dim(covered, group * group_rows, group_rows, 0)
    inputs = jnp.where(covered[:, None], placed, seq_text)

    by_rank = columns.reshape(groups, mps, local_rows, -1).swapaxes(0, 1).reshape(total, -1)
    projected = lax.all_to_all(by_rank, rank, 0, 1, tiled=True)

    up = summed_share(inputs, lambda rows: matmul(rows, up_weight))
    gate = summed_share(inputs, lambda rows: matmul(rows, gate_weight))
    gate_grad, up_grad = unit_grads(gate, up, hidden_grad)

    def back(gate_rows, up_rows):
        return (matmul_t(gate_rows, gate_weight) + matmul_t(up_rows, up_weight)).astype(bf16)

    if dps == 2:
        gate_other, up_other = swap_dp(gate_grad), swap_dp(up_grad)
        mine = back(gate_grad, up_grad)
        other = back(gate_other, up_other)
        partial = jnp.where(
            dp == 0, jnp.concatenate([mine, other], 0), jnp.concatenate([other, mine], 0)
        )
    else:
        partial = back(
            lax.all_gather(gate_grad, "dp", axis=0, tiled=True),
            lax.all_gather(up_grad, "dp", axis=0, tiled=True),
        )
    share = local_cols // mps
    shares = lax.all_to_all(
        partial.reshape(group_rows, mps, share).swapaxes(0, 1), "mp", 0, 0, tiled=True
    )
    grads = jnp.sum(shares.astype(f32), axis=0).astype(bf16)

    grads_all = lax.all_gather(grads, "group", axis=0, tiled=True)
    target, valid = image_targets(
        image_counts,
        image_sequence,
        image_offsets,
        TOK_DEV,
        group * group_rows,
        group_rows,
    )
    rows = jnp.where(valid[:, None], jnp.take(grads_all, target, axis=0), jnp.zeros((), bf16))
    row_grads = lax.all_to_all(rows, "mp", 0, 1, tiled=True)
    sequence_grads = lax.all_to_all(grads, "mp", 0, 1, tiled=True)
    return (projected, sequence_grads, row_grads)


def solution(mesh):
    sizes = tuple(mesh.shape[a] for a in ("group", "dp", "mp"))
    return jax.shard_map(
        functools.partial(local, sizes),
        mesh=mesh,
        in_specs=(
            P(("group", "mp"), "dp"),
            P("dp"),
            P("dp"),
            P("dp", ("group", "mp")),
            P(("group", "mp")),
            P(("group", "mp"), "dp"),
            P("dp"),
            P(("group", "mp"), "dp"),
            P(("group", "mp"), "dp"),
            P("dp", "mp"),
            P("dp", "mp"),
            P("mp", "dp"),
            P(),
            P(),
            P(),
        ),
        out_specs=(P(("group", "mp"), "dp"), P(("group", "mp"), "dp"), P(("group", "mp"), "dp")),
        check_vma=False,
    )
```

```python
import functools

import jax
import jax.numpy as jnp
from jax import lax
from jax.experimental import pallas as pl
from jax.experimental.pallas import tpu as pltpu
from jax.sharding import PartitionSpec as P

TOK_DEV = 128


def seq_sources(counts, sequence, offsets, length, first, count):
    starts = jnp.cumsum(counts) - counts
    rows = first + jnp.arange(count, dtype=jnp.int32)
    seq = rows // length
    pos = rows % length
    hit = (
        (sequence[None, :] == seq[:, None])
        & (offsets[None, :] <= pos[:, None])
        & (pos[:, None] < (offsets + counts)[None, :])
    )
    source = jnp.sum(jnp.where(hit, starts[None, :] + pos[:, None] - offsets[None, :], 0), axis=1)
    return (source, jnp.any(hit, axis=1))


def image_targets(counts, sequence, offsets, length, first, count):
    starts = jnp.cumsum(counts) - counts
    rows = first + jnp.arange(count, dtype=jnp.int32)
    hit = (starts[None, :] <= rows[:, None]) & (rows[:, None] < (starts + counts)[None, :])
    target = jnp.sum(
        jnp.where(
            hit, sequence[None, :] * length + offsets[None, :] + rows[:, None] - starts[None, :], 0
        ),
        axis=1,
    )
    return (target, jnp.any(hit, axis=1))


def unit_grads(gate, up, hidden_grad):
    sig = jax.nn.sigmoid(gate)
    gate_grad = (hidden_grad * up * sig * (1.0 + gate * (1.0 - sig))).astype(jnp.bfloat16)
    up_grad = (hidden_grad * gate * sig).astype(jnp.bfloat16)
    return (gate_grad, up_grad)


def gather_kernel(groups, mps, x_ref, out_ref, local_sem, send_sem, recv_sem):
    g, m = lax.axis_index("group"), lax.axis_index("mp")
    gx = g + 1 - 2 * (g % 2)
    gy = g + 2 - 4 * (g // 2)
    gd = 3 - g
    rows, width = x_ref.shape
    cut, half = rows - rows // 4, width // 2
    head, tail = pl.ds(0, cut), pl.ds(cut, rows - cut)
    every, left, right = pl.ds(0, width), pl.ds(0, half), pl.ds(half, width - half)
    slots, sent = {}, []
    to_x, to_y = {"group": gx}, {"group": gy}
    low, high = {"mp": m - 1}, {"mp": m + 1}

    def slot(key):
        return slots.setdefault(key, len(slots))

    def send(key, owner, line, part, cols, target, when=None, own=False):
        dst = out_ref.at[owner, line, part, cols]
        copy = pltpu.make_async_remote_copy(
            src_ref=x_ref.at[part, cols] if own else dst,
            dst_ref=dst,
            send_sem=send_sem.at[slot(key)],
            recv_sem=recv_sem.at[slot(key)],
            device_id=target,
            device_id_type=pl.DeviceIdType.MESH,
        )
        guarded(when, copy.start)
        sent.append((when, copy))

    def arrive(key, owner, line, part, cols, source, when=None):
        dst = out_ref.at[owner, line, part, cols]
        copy = pltpu.make_async_remote_copy(
            src_ref=dst,
            dst_ref=dst,
            send_sem=send_sem.at[slot(key)],
            recv_sem=recv_sem.at[slot(key)],
            device_id=source,
            device_id_type=pl.DeviceIdType.MESH,
        )
        guarded(when, copy.wait_recv)

    def guarded(when, act):
        if when is None:
            act()
        else:
            pl.when(when)(lambda: act())

    barrier = pltpu.get_barrier_semaphore()
    has_low, has_high = m > 0, m < mps - 1

    def greet(target):
        pl.semaphore_signal(
            barrier, inc=1, device_id=target, device_id_type=pl.DeviceIdType.MESH
        )

    greet(to_x)
    greet(to_y)
    guarded(has_low, lambda: greet(low))
    guarded(has_high, lambda: greet(high))
    pl.semaphore_wait(barrier, 2 + (m + mps - 1) // mps + (2 * mps - 2 - m) // mps)

    keep = pltpu.make_async_copy(x_ref, out_ref.at[g, m], local_sem)
    keep.start()
    send(("up", 0), g, m, head, every, high, has_high, True)
    send(("down", 0), g, m, head, every, low, has_low, True)
    send("tail_x", g, m, tail, every, to_x, None, True)
    send("tail_y", g, m, tail, every, to_y, None, True)
    send(("x", 0, 0), g, m, head, every, to_x, None, True)
    send(("y", 0, 0), g, m, head, every, to_y, None, True)
    send(("up", 0, 0), g, m, tail, every, high, has_high, True)
    send(("down", 0, 0), g, m, tail, every, low, has_low, True)

    arrive("tail_x", gx, m, tail, every, to_x)
    send("tail_xy", gx, m, tail, left, to_y)
    arrive("tail_y", gy, m, tail, every, to_y)
    send("tail_yx", gy, m, tail, right, to_x)
    for owner, j in ((gx, 1), (gy, 2)):
        send(("up", 0, j), owner, m, tail, every, high, has_high)
        send(("down", 0, j), owner, m, tail, every, low, has_low)
    arrive("tail_xy", gd, m, tail, left, to_y)
    arrive("tail_yx", gd, m, tail, right, to_x)
    send(("up", 0, 3), gd, m, tail, every, high, has_high)
    send(("down", 0, 3), gd, m, tail, every, low, has_low)

    def turn(key, line, when=None):
        arrive(("x",) + key, gx, line, head, every, to_x, when)
        send(("xy",) + key, gx, line, head, left, to_y, when)
        arrive(("y",) + key, gy, line, head, every, to_y, when)
        send(("yx",) + key, gy, line, head, right, to_x, when)

    turn((0, 0), m)
    lines = [((0, 0), m, None)]
    for step in range(1, mps):
        ways = (
            ("up", m - step, m >= step, low, high, (m >= step) & has_high),
            ("down", m + step, m < mps - step, high, low, (m < mps - step) & has_low),
        )
        for name, line, come, source, target, on in ways:
            arrive((name, step - 1), g, line, head, every, source, come)
            if step < mps - 1:
                send((name, step), g, line, head, every, target, on)
            send(("x", name, step), g, line, head, every, to_x, come)
            send(("y", name, step), g, line, head, every, to_y, come)
        for name, line, come, source, target, on in ways:
            for owner, j in ((g, 0), (gx, 1), (gy, 2), (gd, 3)):
                arrive((name, step - 1, j), owner, line, tail, every, source, come)
                if step < mps - 1:
                    send((name, step, j), owner, line, tail, every, target, on)
        for name, line, come, source, target, on in ways:
            turn((name, step), line, come)
            lines.append(((name, step), line, come))
    for key, line, come in lines:
        arrive(("xy",) + key, gd, line, head, left, to_y, come)
        arrive(("yx",) + key, gd, line, head, right, to_x, come)
    for when, copy in sent:
        guarded(when, copy.wait_send)
    keep.wait()


def gather_blocks(value, groups, mps, ident):
    rows, width = value.shape
    if groups != 4 or mps < 2 or rows % 64 or width % 256:
        whole = lax.all_gather(value, ("group", "mp"), axis=0, tiled=False)
        return whole.reshape(groups, mps, rows, width)
    count = 4 + 2 * (mps - 1) * 5 + 4 * (2 * mps - 1)
    return pl.pallas_call(
        functools.partial(gather_kernel, groups, mps),
        out_shape=jax.ShapeDtypeStruct((groups, mps, rows, width), value.dtype),
        in_specs=[pl.BlockSpec(memory_space=pl.ANY)],
        out_specs=pl.BlockSpec(memory_space=pl.ANY),
        scratch_shapes=[
            pltpu.SemaphoreType.DMA(()),
            pltpu.SemaphoreType.DMA((count,)),
            pltpu.SemaphoreType.DMA((count,)),
        ],
        compiler_params=pltpu.CompilerParams(collective_id=ident, has_side_effects=True),
        cost_estimate=pl.CostEstimate(
            flops=0, bytes_accessed=2 * groups * mps * rows * width * 2, transcendentals=0
        ),
    )(value)


def swap_dp(value):
    return lax.ppermute(value, "dp", [(0, 1), (1, 0)])


def half_rows(value, part):
    rows = value.shape[0] // 2
    return lax.dynamic_slice_in_dim(value, part * rows, rows, 0)


def local(
    sizes,
    patches,
    norm_gain,
    norm_bias,
    proj_in,
    proj_in_bias,
    proj_out,
    proj_out_bias,
    text_rows,
    out_grads,
    gate_weight,
    up_weight,
    down_weight,
    image_counts,
    image_sequence,
    image_offsets,
):
    groups, dps, mps = sizes
    devices = groups * mps
    local_rows, local_cols = text_rows.shape
    total = local_rows * devices
    group_rows = local_rows * mps
    group, dp, mp = (lax.axis_index(a) for a in ("group", "dp", "mp"))
    bf16, f32 = jnp.bfloat16, jnp.float32
    rank = ("mp", "group")

    block = local_cols // devices
    out_cols = lax.all_to_all(proj_out, rank, 1, 0, tiled=True)
    out_cols = lax.all_gather(out_cols, "dp", axis=1, tiled=True)
    out_bias = lax.dynamic_slice_in_dim(proj_out_bias, (mp * groups + group) * block, block, 0)
    out_bias = lax.all_gather(out_bias, "dp", axis=0, tiled=True)

    seq_text, seq_cotangent = (
        lax.all_gather(text_rows, "mp", axis=0, tiled=True),
        lax.all_gather(out_grads, "mp", axis=0, tiled=True),
    )

    values = patches.astype(f32)
    mean = lax.psum(jnp.sum(values, axis=1), "dp") / (patches.shape[1] * dps)
    centred = values - mean[:, None]
    spread = lax.psum(jnp.sum(centred * centred, axis=1), "dp") / (patches.shape[1] * dps)
    normed = (centred * lax.rsqrt(spread + 1e-05)[:, None] * norm_gain + norm_bias).astype(bf16)
    normed_all = gather_blocks(normed, groups, mps, 0).reshape(total, -1)

    def matmul(a, b):
        return jnp.dot(a, b, preferred_element_type=f32)

    def matmul_t(a, b):
        return lax.dot_general(a, b, (((1,), (1,)), ((), ())), preferred_element_type=f32)

    def summed_share(value, op):
        if dps == 2:
            arriving = swap_dp(op(half_rows(value, 1 - dp)))
            return op(half_rows(value, dp)) + arriving
        return lax.psum_scatter(op(value), "dp", scatter_dimension=0, tiled=True)

    first = summed_share(normed_all, lambda rows: matmul(rows, proj_in))
    activated = jax.nn.gelu(first + proj_in_bias, approximate=False).astype(bf16)
    activated, seq_text, seq_cotangent = lax.optimization_barrier(
        (activated, seq_text, seq_cotangent)
    )
    activated_all = gather_blocks(activated, groups, mps, 1).transpose(2, 1, 0, 3)
    activated_all = activated_all.reshape(activated.shape[0], -1)
    hidden_grad = summed_share(seq_cotangent, lambda rows: matmul_t(rows, down_weight))
    columns = (matmul(activated_all, out_cols) + out_bias).astype(bf16)
    columns = lax.all_to_all(columns, "dp", 1, 0, tiled=True)

    source, covered = seq_sources(
        image_counts, image_sequence, image_offsets, TOK_DEV, 0, total
    )
    placed = jnp.take(columns, source, axis=0)
    placed = lax.all_to_all(placed, "group", 0, 1, tiled=True)
    placed = lax.all_gather(placed, "mp", axis=1, tiled=True)
    covered = lax.dynamic_slice_in_dim(covered, group * group_rows, group_rows, 0)
    inputs = jnp.where(covered[:, None], placed, seq_text)

    by_rank = columns.reshape(groups, mps, local_rows, -1).swapaxes(0, 1).reshape(total, -1)
    projected = lax.all_to_all(by_rank, rank, 0, 1, tiled=True)

    up = summed_share(inputs, lambda rows: matmul(rows, up_weight))
    gate = summed_share(inputs, lambda rows: matmul(rows, gate_weight))
    gate_grad, up_grad = unit_grads(gate, up, hidden_grad)

    def back(gate_rows, up_rows):
        return (matmul_t(gate_rows, gate_weight) + matmul_t(up_rows, up_weight)).astype(bf16)

    if dps == 2:
        gate_other, up_other = swap_dp(gate_grad), swap_dp(up_grad)
        mine = back(gate_grad, up_grad)
        other = back(gate_other, up_other)
        partial = jnp.where(
            dp == 0, jnp.concatenate([mine, other], 0), jnp.concatenate([other, mine], 0)
        )
    else:
        partial = back(
            lax.all_gather(gate_grad, "dp", axis=0, tiled=True),
            lax.all_gather(up_grad, "dp", axis=0, tiled=True),
        )
    share = local_cols // mps
    shares = lax.all_to_all(
        partial.reshape(group_rows, mps, share).swapaxes(0, 1), "mp", 0, 0, tiled=True
    )
    grads = jnp.sum(shares.astype(f32), axis=0).astype(bf16)

    grads_all = lax.all_gather(grads, "group", axis=0, tiled=True)
    target, valid = image_targets(
        image_counts,
        image_sequence,
        image_offsets,
        TOK_DEV,
        group * group_rows,
        group_rows,
    )
    rows = jnp.where(valid[:, None], jnp.take(grads_all, target, axis=0), jnp.zeros((), bf16))
    row_grads = lax.all_to_all(rows, "mp", 0, 1, tiled=True)
    sequence_grads = lax.all_to_all(grads, "mp", 0, 1, tiled=True)
    return (projected, sequence_grads, row_grads)


def solution(mesh):
    sizes = tuple(mesh.shape[a] for a in ("group", "dp", "mp"))
    return jax.shard_map(
        functools.partial(local, sizes),
        mesh=mesh,
        in_specs=(
            P(("group", "mp"), "dp"),
            P("dp"),
            P("dp"),
            P("dp", ("group", "mp")),
            P(("group", "mp")),
            P(("group", "mp"), "dp"),
            P("dp"),
            P(("group", "mp"), "dp"),
            P(("group", "mp"), "dp"),
            P("dp", "mp"),
            P("dp", "mp"),
            P("mp", "dp"),
            P(),
            P(),
            P(),
        ),
        out_specs=(P(("group", "mp"), "dp"), P(("group", "mp"), "dp"), P(("group", "mp"), "dp")),
        check_vma=False,
    )
```
